128 devices in a mesh: row: 4 (over z), col: 32 (over x, y, core).
Axes of the slice: x: 4, y: 4, z: 4, core: 2. Of those that a mesh axis runs over, the one named last changes fastest.
Arguments:
- object_field: float32 [2, 4, 1024, 8192], P(None, None, 'row', 'col'), may hold values from -4 to 4
- probe: float32 [2, 4, 128, 128], replicated, may hold values from -6 to 6
- amplitudes: float32 [4, 32, 5, 128, 128], P('row', 'col'), may hold values from 0.2 to 4
- offsets: int32 [4, 32, 5, 2], P('row', 'col'), may hold values from 0 to 8064, as said below
- counts: int32 [4, 32], P('row', 'col'), may hold values from 1 to 5, as said below
Outputs:
- new_object: float32 [2, 4, 1024, 8192], P(None, None, 'row', 'col')
- new_probe: float32 [2, 4, 128, 128], replicated
The draws below stay inside these ranges and needn't reach their ends.
Inputs may be any that keep to these rules, and one draw needn't show every extreme that they name: `offsets`: slot k of device (a, b) has corner (y, x) with a * 256 <= y < (a + 1) * 256, b * 256 <= x < (b + 1) * 256, y <= 896 and x <= 8064; dead slots hold such corners too. Slots k >= counts of a device are dead; some device has all 5 slots live.
All inputs are finite; a program needn't handle non-finite values.
Results may differ from the reference program's by a relative error of at most 0.00019.
Values sent between devices are 32-bit elements; how exact they have to be, the bound alone decides.
No kernel may reach another device: no remote copies, remote signals or barrier semaphores. Data moves between devices by JAX's collectives and lax.ppermute only.
A program may use at most 128 MiB of HBM per device.

```python
import math
import jax
import jax.numpy as jnp
from jax import lax

P_SIZE = 128
MODES = 4
SLICES = 4
TR = 256
TC = 256
CAP = 5
NR = 1024
NC = 8192
N_ROW = 4
N_COL = 32


def draw_offsets(key, part):
    key = jax.random.fold_in(key, 11)
    key_rows, key_cols = jax.random.split(key)
    band_rows = NR // TR
    band_cols = NC // TC
    row_band = jnp.arange(band_rows, dtype=jnp.int32)[:, None, None]
    col_band = jnp.arange(band_cols, dtype=jnp.int32)[None, :, None]
    row_room = jnp.minimum(TR, NR - P_SIZE - row_band * TR + 1)
    col_room = jnp.minimum(TC, NC - P_SIZE - col_band * TC + 1)
    row_pick = jax.random.randint(key_rows, (band_rows, band_cols, CAP), 0, row_room)
    col_pick = jax.random.randint(key_cols, (band_rows, band_cols, CAP), 0, col_room)
    corners = jnp.stack([row_band * TR + row_pick, col_band * TC + col_pick], axis=-1).astype(jnp.int32)
    corners = corners.at[0, 0, 0].set(jnp.array([0, 0], jnp.int32))
    corners = corners.at[band_rows - 1, band_cols - 1, 0].set(jnp.array([NR - P_SIZE, NC - P_SIZE], jnp.int32))
    return corners.astype(jnp.int32)


def draw_counts(key, part):
    key = jax.random.fold_in(key, 12)
    key_base, key_full = jax.random.split(key)
    band_rows = NR // TR
    band_cols = NC // TC
    base_counts = jax.random.randint(key_base, (band_rows * band_cols,), 1, CAP + 1)
    full_device = jax.random.randint(key_full, (), 0, band_rows * band_cols)
    device_ids = jnp.arange(band_rows * band_cols, dtype=jnp.int32)
    filled = jnp.where(device_ids == full_device, CAP, base_counts)
    return filled.reshape(band_rows, band_cols).astype(jnp.int32)


def shard_levels(rng, extent, cuts, low, largest):
    factor_of, own = 1.0, jax.random.fold_in(rng, 6)
    for dim, parts in cuts:
        heights = jnp.exp(jax.random.uniform(jax.random.fold_in(own, dim), (parts,), jnp.float32, low / len(cuts), largest / len(cuts)))
        factor_of = factor_of * jnp.repeat(heights, extent[dim] // parts).reshape([-1 if axis == dim else 1 for axis in range(len(extent))])
    return factor_of


def gaussian(key, shape, deviation, reach, pieces=(), held_as=jnp.bfloat16):
    values = jax.random.normal(key, shape, jnp.float32) * deviation
    if len(pieces) > 0:
        values = shard_levels(key, shape, pieces, -0.22, 0.18) * values
    return jnp.clip(values, min=-reach, max=reach).astype(held_as)


def setup_inputs(seed: int = 0) -> dict:
    streams_of = jax.random.split(jax.random.key(seed), 6)
    return {
        "object_field": gaussian(streams_of[0], (2, SLICES, NR, NC), 0.6, 4.0, ((2, 4), (3, 32)), jnp.float32),
        "probe": gaussian(streams_of[1], (2, MODES, P_SIZE, P_SIZE), 1.0, 6.0, (), jnp.float32),
        "amplitudes": jnp.clip(jnp.exp(math.log(4.0) - 2.9957323 * jax.random.uniform(streams_of[2], (N_ROW, N_COL, CAP, P_SIZE, P_SIZE), jnp.float32) ** shard_levels(streams_of[2], (N_ROW, N_COL, CAP, P_SIZE, P_SIZE), ((0, 4), (1, 32)), -0.2, 0.2)), 0.2, 4.0),
        "offsets": draw_offsets(jax.random.fold_in(streams_of[5], 71), 0),
        "counts": draw_counts(jax.random.fold_in(streams_of[5], 71), 0),
    }


FRESNEL = 4.0
STEP_OBJECT = 0.5
STEP_PROBE = 0.5

def transfer_kernel(points):
    frequency = jnp.fft.fftfreq(points).astype(jnp.float32)
    phase = -jnp.pi * FRESNEL * (frequency[:, None] ** 2 + frequency[None, :] ** 2)
    return lax.complex(jnp.cos(phase), jnp.sin(phase))

def position_loss(window, probe, amplitude, kernel):
    object_slices = lax.complex(window[0], window[1])
    wavefield = lax.complex(probe[0], probe[1])
    for slice_index in range(SLICES):
        wavefield = wavefield * object_slices[slice_index]
        if slice_index < SLICES - 1:
            spectrum = jnp.fft.fft2(wavefield, norm='ortho') * kernel
            wavefield = jnp.fft.ifft2(spectrum, norm='ortho')
    far_field = jnp.fft.fft2(wavefield, norm='ortho')
    intensity = lax.optimization_barrier(jnp.sum(jnp.real(far_field) ** 2 + jnp.imag(far_field) ** 2, axis=0))
    return jnp.sum((jnp.sqrt(intensity + 1.0) - amplitude) ** 2)

def reference(object_field, probe, amplitudes, offsets, counts):
    kernel = transfer_kernel(P_SIZE)
    flat_offsets = offsets.reshape(-1, 2).astype(jnp.int32)
    flat_amplitudes = amplitudes.reshape(-1, P_SIZE, P_SIZE)
    live_slots = (jnp.arange(CAP, dtype=jnp.int32)[None, None, :] < counts[:, :, None]).reshape(-1).astype(jnp.float32)
    zero_index = jnp.zeros((), jnp.int32)

    def accumulate(carry, item):
        grad_object, grad_probe, weight = carry
        position, amplitude, alive = item
        starts = (zero_index, zero_index, position[0], position[1])
        window = lax.dynamic_slice(object_field, starts, (2, SLICES, P_SIZE, P_SIZE))

        def local_loss(window_part, probe_part):
            return position_loss(window_part, probe_part, amplitude, kernel)
        loss_value, pull_back = jax.vjp(local_loss, window, probe)
        grad_window, grad_wave = pull_back(alive)
        previous = lax.dynamic_slice(grad_object, starts, (2, SLICES, P_SIZE, P_SIZE))
        grad_object = lax.dynamic_update_slice(grad_object, previous + grad_window, starts)
        weight = weight + alive * (window[0, 0] ** 2 + window[1, 0] ** 2)
        return ((grad_object, grad_probe + grad_wave, weight), None)
    initial = (jnp.zeros_like(object_field), jnp.zeros_like(probe), jnp.zeros((P_SIZE, P_SIZE), jnp.float32))
    totals, unused = lax.scan(accumulate, initial, (flat_offsets, flat_amplitudes, live_slots))
    grad_object, grad_probe, weight = totals
    new_object = object_field - STEP_OBJECT * grad_object
    new_probe = probe - STEP_PROBE * grad_probe / (weight + 1.0)
    return (new_object, new_probe)
```

```python
from functools import partial
import math

import jax
import jax.numpy as jnp
import ml_dtypes
import numpy as np
from jax import lax
from jax.experimental import pallas as pl
from jax.experimental.pallas import tpu as pltpu
from jax.sharding import PartitionSpec as P

FRESNEL = 4.0
STEP_OBJECT = 0.5
STEP_PROBE = 0.5
AXES = ("row", "col")
N = 128
MODES = 4
EXT = 384
TILE = 256
VMEM_LIMIT = 50 * 1024 * 1024


def split_np(matrix):
    high = matrix.astype(np.float32).astype(ml_dtypes.bfloat16)
    low = (matrix - high.astype(np.float64)).astype(np.float32).astype(ml_dtypes.bfloat16)
    return np.stack([high, low])


def tables_np():
    position = np.arange(N)
    dft = np.exp(-2j * np.pi * (np.outer(position, position) % N) / N) / math.sqrt(N)
    frequency = np.where(position < N // 2, position, position - N) / N
    chirp = np.exp(-1j * np.pi * FRESNEL * frequency**2)
    propagator = dft.conj() @ (chirp[:, None] * dft)
    propagator = 0.5 * (propagator + propagator.T)
    out = []
    for matrix in (propagator, dft):
        real, imag = matrix.real, matrix.imag
        out.append(
            np.stack(
                [
                    split_np(np.block([[real, imag], [-imag, real]])),
                    split_np(np.block([[real, -imag], [imag, real]])),
                ]
            )
        )
    return np.stack(out)


def split(value):
    high = value.astype(jnp.bfloat16)
    low = (value - high.astype(jnp.float32)).astype(jnp.bfloat16)
    return high, low


def dot(left, right):
    return jnp.dot(left, right, preferred_element_type=jnp.float32)


def mode(value, index):
    return value[index * N : (index + 1) * N]


def sandwich(real, imag, tables, which, conj):
    right_form, left_form = (1, 0) if conj else (0, 1)
    high, low = split(jnp.concatenate([real, imag], axis=1))
    table_high, table_low = tables[which, right_form, 0], tables[which, right_form, 1]
    mixed = dot(high, table_high) + dot(low, table_high) + dot(high, table_low)
    mixed = jnp.concatenate(
        [
            jnp.concatenate([mode(mixed, m)[:, :N] for m in range(MODES)], axis=1),
            jnp.concatenate([mode(mixed, m)[:, N:] for m in range(MODES)], axis=1),
        ],
        axis=0,
    )
    high, low = split(mixed)
    table_high, table_low = tables[which, left_form, 0], tables[which, left_form, 1]
    out = dot(table_high, high) + dot(table_high, low) + dot(table_low, high)
    return (
        jnp.concatenate([out[:N, m * N : (m + 1) * N] for m in range(MODES)], axis=0),
        jnp.concatenate([out[N:, m * N : (m + 1) * N] for m in range(MODES)], axis=0),
    )


def spread(value):
    return jnp.concatenate([value] * MODES, axis=0)


def times(real, imag, other_real, other_imag):
    other_real, other_imag = spread(other_real), spread(other_imag)
    return real * other_real - imag * other_imag, real * other_imag + imag * other_real


def times_conj(real, imag, other_real, other_imag):
    other_real, other_imag = spread(other_real), spread(other_imag)
    return real * other_real + imag * other_imag, imag * other_real - real * other_imag


def sum_modes(value):
    return (mode(value, 0) + mode(value, 1)) + (mode(value, 2) + mode(value, 3))


def slice_gradient(wave_real, wave_imag, grad_real, grad_imag):
    return (
        sum_modes(wave_real * grad_real + wave_imag * grad_imag),
        sum_modes(wave_real * grad_imag - wave_imag * grad_real),
    )


def corner_of(place, slot):
    row, col = place[slot, 0], place[slot, 1]
    tile = jnp.where(col >= N, 1, 0)
    return row, tile, col - tile * N


def cut(ext, part, depth, where):
    row, tile, turn = where
    block = jnp.concatenate([ext[part, depth, tile + k, pl.ds(row, N), :] for k in range(2)], axis=1)
    return pltpu.roll(block, lax.rem(2 * N - turn, 2 * N), 1)[:, :N]


def deposit(ext, part, depth, where, value):
    row, tile, turn = where
    block = pltpu.roll(jnp.concatenate([value, jnp.zeros_like(value)], axis=1), turn, 1)
    for k in range(2):
        ext[part, depth, tile + k, pl.ds(row, N), :] += block[:, k * N : (k + 1) * N]


def run_copies(pairs, sems):
    copies = [pltpu.make_async_copy(*pair, sems.at[k]) for k, pair in enumerate(pairs)]
    for copy in copies:
        copy.start()
    for copy in copies:
        copy.wait()


def load_extended(first, own, bottom, right, corner, ext, sems):
    upper, lower = pl.ds(0, TILE), pl.ds(TILE, N)
    pairs = []
    for k in range(2):
        lanes = pl.ds(k * N, N)
        pairs.append((own.at[:, pl.ds(first, 2), :, lanes], ext.at[:, :, k, upper]))
        pairs.append((bottom.at[:, :, :, lanes], ext.at[:, :, k, lower]))
    pairs.append((right, ext.at[:, :, 2, upper]))
    pairs.append((corner, ext.at[:, :, 2, lower]))
    run_copies(pairs, sems)


def store_gradient(ext, own, bottom, right, sems):
    pairs = []
    for k in range(2):
        lanes = pl.ds(k * N, N)
        pairs.append((ext.at[:, :, k, pl.ds(0, TILE)], own.at[:, :, :, lanes]))
        pairs.append((ext.at[:, :, k, pl.ds(TILE, N)], bottom.at[:, :, :, lanes]))
    pairs.append((ext.at[:, :, 2], right))
    run_copies(pairs, sems)


def first_half(place, count, own, bottom, right, corner, probe, tables, windows, wave1, wave2, weight, ext, sems):
    slot = pl.program_id(0)

    @pl.when(slot == 0)
    def _():
        load_extended(0, own, bottom, right, corner, ext, sems)
        weight[...] = jnp.zeros_like(weight)

    @pl.when(slot < count[0])
    def _():
        where = corner_of(place, slot)
        real, imag = probe[0], probe[1]
        for depth in range(2):
            cut_real, cut_imag = cut(ext, 0, depth, where), cut(ext, 1, depth, where)
            windows[0, 0, depth] = cut_real
            windows[0, 1, depth] = cut_imag
            if depth == 0:
                weight[...] += cut_real * cut_real + cut_imag * cut_imag
            real, imag = sandwich(*times(real, imag, cut_real, cut_imag), tables, 0, False)
            out = (wave1, wave2)[depth]
            out[0, 0] = real
            out[0, 1] = imag


def second_half(
    place, count, own, bottom, right, corner, wave2, amplitude, tables, grad2, grad_own, grad_bottom, grad_right, ext, grad, sems
):
    slot = pl.program_id(0)

    @pl.when(slot == 0)
    def _():
        load_extended(2, own, bottom, right, corner, ext, sems)
        grad[...] = jnp.zeros_like(grad)

    @pl.when(slot < count[0])
    def _():
        where = corner_of(place, slot)
        object2 = cut(ext, 0, 0, where), cut(ext, 1, 0, where)
        object3 = cut(ext, 0, 1, where), cut(ext, 1, 1, where)
        wave3 = sandwich(*times(wave2[0, 0], wave2[0, 1], *object2), tables, 0, False)
        real, imag = sandwich(*times(*wave3, *object3), tables, 1, False)
        scale = jnp.sqrt(sum_modes(real * real + imag * imag) + 1.0)
        factor = spread(2.0 - 2.0 * (amplitude[0] / scale))
        real, imag = sandwich(real * factor, imag * factor, tables, 1, True)
        slice_real, slice_imag = slice_gradient(*wave3, real, imag)
        deposit(grad, 0, 1, where, slice_real)
        deposit(grad, 1, 1, where, slice_imag)
        real, imag = sandwich(*times_conj(real, imag, *object3), tables, 0, True)
        slice_real, slice_imag = slice_gradient(wave2[0, 0], wave2[0, 1], real, imag)
        deposit(grad, 0, 0, where, slice_real)
        deposit(grad, 1, 0, where, slice_imag)
        real, imag = times_conj(real, imag, *object2)
        grad2[0, 0] = real
        grad2[0, 1] = imag

    @pl.when(slot == pl.num_programs(0) - 1)
    def _():
        store_gradient(grad, grad_own, grad_bottom, grad_right, sems)


def third_part(place, count, windows, wave1, grad2, probe, tables, grad_probe, grad_own, grad_bottom, grad_right, grad, sems):
    slot = pl.program_id(0)

    @pl.when(slot == 0)
    def _():
        grad[...] = jnp.zeros_like(grad)
        grad_probe[...] = jnp.zeros_like(grad_probe)

    @pl.when(slot < count[0])
    def _():
        where = corner_of(place, slot)
        real, imag = sandwich(grad2[0, 0], grad2[0, 1], tables, 0, True)
        slice_real, slice_imag = slice_gradient(wave1[0, 0], wave1[0, 1], real, imag)
        deposit(grad, 0, 1, where, slice_real)
        deposit(grad, 1, 1, where, slice_imag)
        real, imag = times_conj(real, imag, windows[0, 0, 1], windows[0, 1, 1])
        real, imag = sandwich(real, imag, tables, 0, True)
        slice_real, slice_imag = slice_gradient(probe[0], probe[1], real, imag)
        deposit(grad, 0, 0, where, slice_real)
        deposit(grad, 1, 0, where, slice_imag)
        real, imag = times_conj(real, imag, windows[0, 0, 0], windows[0, 1, 0])
        grad_probe[0] += real
        grad_probe[1] += imag

    @pl.when(slot == pl.num_programs(0) - 1)
    def _():
        store_gradient(grad, grad_own, grad_bottom, grad_right, sems)


def f32(*shape):
    return jax.ShapeDtypeStruct(shape, jnp.float32)


def whole(*shape):
    return pl.BlockSpec(shape, lambda slot: (0,) * len(shape))


def per_slot(*shape):
    return pl.BlockSpec((1, *shape), lambda slot: (slot,) + (0,) * len(shape))


SMEM = pl.BlockSpec(memory_space=pltpu.SMEM)
HBM = pl.BlockSpec(memory_space=pl.ANY)
PARAMS = pltpu.CompilerParams(vmem_limit_bytes=VMEM_LIMIT, dimension_semantics=("arbitrary",))
TABLES = whole(2, 2, 2, 2 * N, 2 * N)
WAVE = (2, MODES * N, N)
EXTENDED = pltpu.VMEM((2, 2, 3, EXT, N), jnp.float32)


def shifted(value, axis, steps):
    count = lax.axis_size(axis)
    leading, last = (max(0, -steps), min(count, count - steps))
    return lax.ppermute(value, axis, [(source, source + steps) for source in range(leading, last)])


def mesh_perm(move):
    pairs = []
    for z in range(4):
        for x in range(4):
            for y in range(4):
                for core in range(2):
                    to_z, to_x, to_y, to_core = move(z, x, y, core)
                    source = z * 32 + (x * 4 + y) * 2 + core
                    pairs.append((source, to_z * 32 + (to_x * 4 + to_y) * 2 + to_core))
    return pairs


SWAP_CORE = mesh_perm(lambda z, x, y, core: (z, x, y, 1 - core))
ALONG_Z = {k: mesh_perm(lambda z, x, y, core, k=k: (z ^ k, x, y, core)) for k in (1, 2, 3)}
ALONG_X = {k: mesh_perm(lambda z, x, y, core, k=k: (z, x ^ k, y, core)) for k in (1, 2, 3)}
ALONG_Y = {k: mesh_perm(lambda z, x, y, core, k=k: (z, x, y ^ k, core)) for k in (1, 2, 3)}


def probe_update(probe, grad_probe, weight):
    z = lax.axis_index("row")
    core = lax.axis_index("col") % 2
    total = jnp.concatenate([grad_probe.reshape(2 * MODES, N, N), weight[None]], axis=0)
    rows = N // 2

    def part(value, index, size):
        return lax.dynamic_slice_in_dim(value, index * size, size, axis=1)

    total = part(total, core, rows) + lax.ppermute(part(total, 1 - core, rows), AXES, SWAP_CORE)
    rows = rows // 4
    arrived = [lax.ppermute(part(total, z ^ k, rows), AXES, ALONG_Z[k]) for k in (1, 2, 3)]
    total = part(total, z, rows) + arrived[0] + arrived[1] + arrived[2]
    for along in (ALONG_Y, ALONG_X):
        place = lax.axis_index("col") // 2
        place = place % 4 if along is ALONG_Y else place // 4
        arrived = [total] + [lax.ppermute(total, AXES, along[k]) for k in (1, 2, 3)]
        total = (arrived[0] + arrived[1]) + (arrived[2] + arrived[3])
    mine = part(probe.reshape(2 * MODES, N, N), core * 4 + z, rows)
    mine = mine - STEP_PROBE * total[: 2 * MODES] / (total[2 * MODES :] + 1.0)
    arrived = [mine] + [lax.ppermute(mine, AXES, ALONG_Z[k]) for k in (1, 2, 3)]
    half = jnp.zeros((2 * MODES, 4 * rows, N), jnp.float32)
    for k in range(4):
        half = lax.dynamic_update_slice_in_dim(half, arrived[k], (z ^ k) * rows, axis=1)
    other = lax.ppermute(half, AXES, SWAP_CORE)
    low = jnp.where(core == 0, half, other)
    high = jnp.where(core == 0, other, half)
    return jnp.concatenate([low, high], axis=1).reshape(probe.shape)


def shards(tables, object_field, probe, amplitudes, offsets, counts):
    row_index = lax.axis_index("row")
    col_index = lax.axis_index("col")
    slots = offsets.shape[2]
    origin = jnp.stack([row_index * TILE, col_index * TILE]).astype(jnp.int32)
    place = offsets[0, 0] - origin[None, :]
    count = counts[0]
    waves = probe.reshape(WAVE)

    bottoms, rights, corners = [], [], []
    for first in (0, 2):
        piece = object_field[:, first : first + 2]
        bottoms.append(shifted(piece[:, :, :N, :], "row", -1))
        rights.append(shifted(piece[:, :, :, :N], "col", -1))
        corners.append(shifted(bottoms[-1][:, :, :, :N], "col", -1))

    windows, wave1, wave2, weight = pl.pallas_call(
        first_half,
        grid=(slots,),
        in_specs=[SMEM, SMEM, HBM, HBM, HBM, HBM, whole(*WAVE), TABLES],
        out_specs=[per_slot(2, 2, N, N), per_slot(*WAVE), per_slot(*WAVE), whole(N, N)],
        out_shape=[f32(slots, 2, 2, N, N), f32(slots, *WAVE), f32(slots, *WAVE), f32(N, N)],
        scratch_shapes=[EXTENDED, pltpu.SemaphoreType.DMA((6,))],
        compiler_params=PARAMS,
        name="first_half",
    )(place, count, object_field, bottoms[0], rights[0], corners[0], waves, tables)

    grad_specs = [HBM, HBM, HBM]
    grad_shapes = [f32(2, 2, TILE, TILE), f32(2, 2, N, TILE), f32(2, 2, EXT, N)]
    grad2, *late = pl.pallas_call(
        second_half,
        grid=(slots,),
        in_specs=[SMEM, SMEM, HBM, HBM, HBM, HBM, per_slot(*WAVE), per_slot(N, N), TABLES],
        out_specs=[per_slot(*WAVE)] + grad_specs,
        out_shape=[f32(slots, *WAVE)] + grad_shapes,
        scratch_shapes=[EXTENDED, EXTENDED, pltpu.SemaphoreType.DMA((6,))],
        compiler_params=PARAMS,
        name="second_half",
    )(place, count, object_field, bottoms[1], rights[1], corners[1], wave2, amplitudes[0, 0], tables)

    grad_probe, *early = pl.pallas_call(
        third_part,
        grid=(slots,),
        in_specs=[SMEM, SMEM, per_slot(2, 2, N, N), per_slot(*WAVE), per_slot(*WAVE), whole(*WAVE), TABLES],
        out_specs=[whole(*WAVE)] + grad_specs,
        out_shape=[f32(*WAVE)] + grad_shapes,
        scratch_shapes=[EXTENDED, pltpu.SemaphoreType.DMA((5,))],
        compiler_params=PARAMS,
        name="third_part",
    )(place, count, windows, wave1, grad2, waves, tables)

    tiles = []
    for first, (own, bottom, right) in ((0, early), (2, late)):
        returned = shifted(right, "col", 1)
        bottom = bottom.at[:, :, :, :N].add(returned[:, :, TILE:])
        back = shifted(bottom, "row", 1)
        own = own.at[:, :, :, :N].add(returned[:, :, :TILE])
        tiles.append(own.at[:, :, :N, :].add(back))
    new_object = object_field - STEP_OBJECT * jnp.concatenate(tiles, axis=1)
    return new_object, probe_update(probe, grad_probe, weight)


def solution(mesh):
    mapped = jax.shard_map(
        shards,
        mesh=mesh,
        in_specs=(
            P(),
            P(None, None, "row", "col"),
            P(),
            P("row", "col", None, None, None),
            P("row", "col", None, None),
            P("row", "col"),
        ),
        out_specs=(P(None, None, "row", "col"), P()),
        check_vma=False,
    )
    return partial(mapped, jnp.asarray(tables_np()))
```

```python
from functools import partial
import math

import jax
import jax.numpy as jnp
import ml_dtypes
import numpy as np
from jax import lax
from jax.experimental import pallas as pl
from jax.experimental.pallas import tpu as pltpu
from jax.sharding import PartitionSpec as P

FRESNEL = 4.0
STEP_OBJECT = 0.5
STEP_PROBE = 0.5
AXES = ("row", "col")
N = 128
MODES = 4
EXT = 384
TILE = 256
VMEM_LIMIT = 50 * 1024 * 1024


def split_np(matrix):
    high = matrix.astype(np.float32).astype(ml_dtypes.bfloat16)
    low = (matrix - high.astype(np.float64)).astype(np.float32).astype(ml_dtypes.bfloat16)
    return np.stack([high, low])


def tables_np():
    position = np.arange(N)
    dft = np.exp(-2j * np.pi * (np.outer(position, position) % N) / N) / math.sqrt(N)
    frequency = np.where(position < N // 2, position, position - N) / N
    chirp = np.exp(-1j * np.pi * FRESNEL * frequency**2)
    propagator = dft.conj() @ (chirp[:, None] * dft)
    propagator = 0.5 * (propagator + propagator.T)
    out = []
    for matrix in (propagator, dft):
        real, imag = matrix.real, matrix.imag
        out.append(
            np.stack(
                [
                    split_np(np.block([[real, imag], [-imag, real]])),
                    split_np(np.block([[real, -imag], [imag, real]])),
                ]
            )
        )
    return np.stack(out)


def split(value):
    high = value.astype(jnp.bfloat16)
    low = (value - high.astype(jnp.float32)).astype(jnp.bfloat16)
    return high, low


def dot(left, right):
    return jnp.dot(left, right, preferred_element_type=jnp.float32)


def sandwich(waves, tables, which, conj):
    right_form, left_form = (1, 0) if conj else (0, 1)
    high, low = tables[which, right_form, 0], tables[which, right_form, 1]
    right = jnp.concatenate([high, high, low], axis=0)
    high, low = tables[which, left_form, 0], tables[which, left_form, 1]
    left = jnp.concatenate([high, high, low], axis=1)
    mixed = []
    for wave in waves:
        high, low = split(jnp.concatenate(wave, axis=1))
        mixed.append(dot(jnp.concatenate([high, low, high], axis=1), right))
    out = []
    for first in range(0, MODES, 2):
        pair = mixed[first : first + 2]
        high, low = split(
            jnp.concatenate(
                [
                    jnp.concatenate([wave[:, :N] for wave in pair], axis=1),
                    jnp.concatenate([wave[:, N:] for wave in pair], axis=1),
                ],
                axis=0,
            )
        )
        operand = jnp.concatenate([high, low, high], axis=0)
        real, imag = dot(left[:N], operand), dot(left[N:], operand)
        out += [(real[:, :N], imag[:, :N]), (real[:, N:], imag[:, N:])]
    return out


def load_waves(ref):
    return [(ref[0, m * N : (m + 1) * N], ref[1, m * N : (m + 1) * N]) for m in range(MODES)]


def store_waves(ref, waves):
    for m, (real, imag) in enumerate(waves):
        ref[0, m * N : (m + 1) * N] = real
        ref[1, m * N : (m + 1) * N] = imag


def times(waves, other):
    a, b = other
    return [(real * a - imag * b, real * b + imag * a) for real, imag in waves]


def times_conj(waves, other):
    a, b = other
    return [(real * a + imag * b, imag * a - real * b) for real, imag in waves]


def sum_modes(terms):
    return (terms[0] + terms[1]) + (terms[2] + terms[3])


def slice_gradient(waves, grads):
    pairs = [(*wave, *grad) for wave, grad in zip(waves, grads)]
    return (
        sum_modes([a * c + b * d for a, b, c, d in pairs]),
        sum_modes([a * d - b * c for a, b, c, d in pairs]),
    )


def corner_of(place, slot):
    row, col = place[slot, 0], place[slot, 1]
    tile = jnp.where(col >= N, 1, 0)
    return row, tile, col - tile * N


def cut(ext, part, depth, where):
    row, tile, turn = where
    block = jnp.concatenate([ext[part, depth, tile + k, pl.ds(row, N), :] for k in range(2)], axis=1)
    return pltpu.roll(block, lax.rem(2 * N - turn, 2 * N), 1)[:, :N]


def deposit(ext, part, depth, where, value):
    row, tile, turn = where
    block = pltpu.roll(jnp.concatenate([value, jnp.zeros_like(value)], axis=1), turn, 1)
    for k in range(2):
        ext[part, depth, tile + k, pl.ds(row, N), :] += block[:, k * N : (k + 1) * N]


def run_copies(pairs, sems):
    copies = [pltpu.make_async_copy(*pair, sems.at[k]) for k, pair in enumerate(pairs)]
    for copy in copies:
        copy.start()
    for copy in copies:
        copy.wait()


def load_extended(first, own, bottom, right, corner, ext, sems):
    upper, lower = pl.ds(0, TILE), pl.ds(TILE, N)
    pairs = []
    for k in range(2):
        lanes = pl.ds(k * N, N)
        pairs.append((own.at[:, pl.ds(first, 2), :, lanes], ext.at[:, :, k, upper]))
        pairs.append((bottom.at[:, :, :, lanes], ext.at[:, :, k, lower]))
    pairs.append((right, ext.at[:, :, 2, upper]))
    pairs.append((corner, ext.at[:, :, 2, lower]))
    run_copies(pairs, sems)


def store_gradient(ext, own, bottom, right, sems):
    pairs = []
    for k in range(2):
        lanes = pl.ds(k * N, N)
        pairs.append((ext.at[:, :, k, pl.ds(0, TILE)], own.at[:, :, :, lanes]))
        pairs.append((ext.at[:, :, k, pl.ds(TILE, N)], bottom.at[:, :, :, lanes]))
    pairs.append((ext.at[:, :, 2], right))
    run_copies(pairs, sems)


def cut_slice(ext, depth, where):
    return cut(ext, 0, depth, where), cut(ext, 1, depth, where)


def deposit_slice(grad, depth, where, value):
    deposit(grad, 0, depth, where, value[0])
    deposit(grad, 1, depth, where, value[1])


def first_half(place, count, own, bottom, right, corner, probe, tables, windows, wave1, wave2, weight, ext, sems):
    slot = pl.program_id(0)

    @pl.when(slot == 0)
    def _():
        load_extended(0, own, bottom, right, corner, ext, sems)
        weight[...] = jnp.zeros_like(weight)

    @pl.when(slot < count[0])
    def _():
        where = corner_of(place, slot)
        waves = load_waves(probe)
        for depth in range(2):
            window = cut_slice(ext, depth, where)
            windows[0, 0, depth], windows[0, 1, depth] = window
            if depth == 0:
                weight[...] += window[0] * window[0] + window[1] * window[1]
            waves = sandwich(times(waves, window), tables, 0, False)
            store_waves((wave1, wave2)[depth].at[0], waves)


def second_half(
    place, count, own, bottom, right, corner, wave2, amplitude, tables, grad2, grad_own, grad_bottom, grad_right, ext, grad, wave3, sems
):
    slot = pl.program_id(0)

    @pl.when(slot == 0)
    def _():
        load_extended(2, own, bottom, right, corner, ext, sems)
        grad[...] = jnp.zeros_like(grad)

    @pl.when(slot < count[0])
    def _():
        where = corner_of(place, slot)
        object2, object3 = cut_slice(ext, 0, where), cut_slice(ext, 1, where)
        waves = sandwich(times(load_waves(wave2.at[0]), object2), tables, 0, False)
        store_waves(wave3, waves)
        far = sandwich(times(waves, object3), tables, 1, False)
        intensity = sum_modes([real * real + imag * imag for real, imag in far])
        factor = 2.0 - 2.0 * (amplitude[0] / jnp.sqrt(intensity + 1.0))
        grads = sandwich([(real * factor, imag * factor) for real, imag in far], tables, 1, True)
        deposit_slice(grad, 1, where, slice_gradient(load_waves(wave3), grads))
        grads = sandwich(times_conj(grads, object3), tables, 0, True)
        deposit_slice(grad, 0, where, slice_gradient(load_waves(wave2.at[0]), grads))
        store_waves(grad2.at[0], times_conj(grads, object2))

    @pl.when(slot == pl.num_programs(0) - 1)
    def _():
        store_gradient(grad, grad_own, grad_bottom, grad_right, sems)


def third_part(place, count, windows, wave1, grad2, probe, tables, grad_probe, grad_own, grad_bottom, grad_right, grad, sems):
    slot = pl.program_id(0)

    @pl.when(slot == 0)
    def _():
        grad[...] = jnp.zeros_like(grad)
        grad_probe[...] = jnp.zeros_like(grad_probe)

    @pl.when(slot < count[0])
    def _():
        where = corner_of(place, slot)
        object0, object1 = [(windows[0, 0, depth], windows[0, 1, depth]) for depth in range(2)]
        grads = sandwich(load_waves(grad2.at[0]), tables, 0, True)
        deposit_slice(grad, 1, where, slice_gradient(load_waves(wave1.at[0]), grads))
        grads = sandwich(times_conj(grads, object1), tables, 0, True)
        deposit_slice(grad, 0, where, slice_gradient(load_waves(probe), grads))
        for m, (real, imag) in enumerate(times_conj(grads, object0)):
            grad_probe[0, m * N : (m + 1) * N] += real
            grad_probe[1, m * N : (m + 1) * N] += imag

    @pl.when(slot == pl.num_programs(0) - 1)
    def _():
        store_gradient(grad, grad_own, grad_bottom, grad_right, sems)


def cost(products):
    flops = products * 5 * 3 * 2 * MODES * N * (2 * N) * (2 * N)
    return pl.CostEstimate(flops=2 * flops, bytes_accessed=8 * 2**20, transcendentals=0)


def f32(*shape):
    return jax.ShapeDtypeStruct(shape, jnp.float32)


def whole(*shape):
    return pl.BlockSpec(shape, lambda slot: (0,) * len(shape))


def per_slot(*shape):
    return pl.BlockSpec((1, *shape), lambda slot: (slot,) + (0,) * len(shape))


SMEM = pl.BlockSpec(memory_space=pltpu.SMEM)
HBM = pl.BlockSpec(memory_space=pl.ANY)
PARAMS = pltpu.CompilerParams(vmem_limit_bytes=VMEM_LIMIT, dimension_semantics=("arbitrary",))
TABLES = whole(2, 2, 2, 2 * N, 2 * N)
WAVE = (2, MODES * N, N)
EXTENDED = pltpu.VMEM((2, 2, 3, EXT, N), jnp.float32)


def shifted(value, axis, steps):
    count = lax.axis_size(axis)
    leading, last = (max(0, -steps), min(count, count - steps))
    return lax.ppermute(value, axis, [(source, source + steps) for source in range(leading, last)])


def mesh_perm(move):
    pairs = []
    for z in range(4):
        for x in range(4):
            for y in range(4):
                for core in range(2):
                    to_z, to_x, to_y, to_core = move(z, x, y, core)
                    source = z * 32 + (x * 4 + y) * 2 + core
                    pairs.append((source, to_z * 32 + (to_x * 4 + to_y) * 2 + to_core))
    return pairs


SWAP_CORE = mesh_perm(lambda z, x, y, core: (z, x, y, 1 - core))
ALONG_Z = {k: mesh_perm(lambda z, x, y, core, k=k: (z ^ k, x, y, core)) for k in (1, 2, 3)}
ALONG_X = {k: mesh_perm(lambda z, x, y, core, k=k: (z, x ^ k, y, core)) for k in (1, 2, 3)}
ALONG_Y = {k: mesh_perm(lambda z, x, y, core, k=k: (z, x, y ^ k, core)) for k in (1, 2, 3)}


QUARTER = N // 8


def part(value, index, size):
    return lax.dynamic_slice_in_dim(value, index * size, size, axis=1)


def share_of_sum(grad_probe, weight):
    z = lax.axis_index("row")
    core = lax.axis_index("col") % 2
    total = jnp.concatenate([grad_probe.reshape(2 * MODES, N, N), weight[None]], axis=0)
    rows = N // 2
    total = part(total, core, rows) + lax.ppermute(part(total, 1 - core, rows), AXES, SWAP_CORE)
    arrived = [lax.ppermute(part(total, z ^ k, QUARTER), AXES, ALONG_Z[k]) for k in (1, 2, 3)]
    return part(total, z, QUARTER) + arrived[0] + arrived[1] + arrived[2]


def sum_plane(total):
    for along in (ALONG_Y, ALONG_X):
        arrived = [total] + [lax.ppermute(total, AXES, along[k]) for k in (1, 2, 3)]
        total = (arrived[0] + arrived[1]) + (arrived[2] + arrived[3])
    return total


def gather_half(probe, total):
    z = lax.axis_index("row")
    core = lax.axis_index("col") % 2
    mine = part(probe.reshape(2 * MODES, N, N), core * 4 + z, QUARTER)
    mine = mine - STEP_PROBE * total[: 2 * MODES] / (total[2 * MODES :] + 1.0)
    arrived = [mine] + [lax.ppermute(mine, AXES, ALONG_Z[k]) for k in (1, 2, 3)]
    half = jnp.zeros((2 * MODES, N // 2, N), jnp.float32)
    for k in range(4):
        half = lax.dynamic_update_slice_in_dim(half, arrived[k], (z ^ k) * QUARTER, axis=1)
    return half


def gather_whole(half):
    core = lax.axis_index("col") % 2
    other = lax.ppermute(half, AXES, SWAP_CORE)
    low = jnp.where(core == 0, half, other)
    high = jnp.where(core == 0, other, half)
    return jnp.concatenate([low, high], axis=1)


def shards(tables, object_field, probe, amplitudes, offsets, counts):
    row_index = lax.axis_index("row")
    col_index = lax.axis_index("col")
    slots = offsets.shape[2]
    origin = jnp.stack([row_index * TILE, col_index * TILE]).astype(jnp.int32)
    place = offsets[0, 0] - origin[None, :]
    count = counts[0]
    waves = probe.reshape(WAVE)

    bottoms, rights, corners = [], [], []
    for first in (0, 2):
        piece = object_field[:, first : first + 2]
        bottoms.append(shifted(piece[:, :, :N, :], "row", -1))
        rights.append(shifted(piece[:, :, :, :N], "col", -1))
        corners.append(shifted(bottoms[-1][:, :, :, :N], "col", -1))

    windows, wave1, wave2, weight = pl.pallas_call(
        first_half,
        grid=(slots,),
        in_specs=[SMEM, SMEM, HBM, HBM, HBM, HBM, whole(*WAVE), TABLES],
        out_specs=[per_slot(2, 2, N, N), per_slot(*WAVE), per_slot(*WAVE), whole(N, N)],
        out_shape=[f32(slots, 2, 2, N, N), f32(slots, *WAVE), f32(slots, *WAVE), f32(N, N)],
        scratch_shapes=[EXTENDED, pltpu.SemaphoreType.DMA((6,))],
        compiler_params=PARAMS,
        cost_estimate=cost(4),
        name="first_half",
    )(place, count, object_field, bottoms[0], rights[0], corners[0], waves, tables)

    grad_specs = [HBM, HBM, HBM]
    grad_shapes = [f32(2, 2, TILE, TILE), f32(2, 2, N, TILE), f32(2, 2, EXT, N)]
    grad2, *late = pl.pallas_call(
        second_half,
        grid=(slots,),
        in_specs=[SMEM, SMEM, HBM, HBM, HBM, HBM, per_slot(*WAVE), per_slot(N, N), TABLES],
        out_specs=[per_slot(*WAVE)] + grad_specs,
        out_shape=[f32(slots, *WAVE)] + grad_shapes,
        scratch_shapes=[EXTENDED, EXTENDED, pltpu.VMEM(WAVE, jnp.float32), pltpu.SemaphoreType.DMA((6,))],
        compiler_params=PARAMS,
        cost_estimate=cost(8),
        name="second_half",
    )(place, count, object_field, bottoms[1], rights[1], corners[1], wave2, amplitudes[0, 0], tables)

    grad_probe, *early = pl.pallas_call(
        third_part,
        grid=(slots,),
        in_specs=[SMEM, SMEM, per_slot(2, 2, N, N), per_slot(*WAVE), per_slot(*WAVE), whole(*WAVE), TABLES],
        out_specs=[whole(*WAVE)] + grad_specs,
        out_shape=[f32(*WAVE)] + grad_shapes,
        scratch_shapes=[EXTENDED, pltpu.SemaphoreType.DMA((5,))],
        compiler_params=PARAMS,
        cost_estimate=cost(4),
        name="third_part",
    )(place, count, windows, wave1, grad2, waves, tables)

    returned_late = shifted(late[2], "col", 1)
    grad_probe, returned_late = lax.optimization_barrier((grad_probe, returned_late))
    back_late = shifted(late[1].at[:, :, :, :N].add(returned_late[:, :, TILE:]), "row", 1)
    returned_early = shifted(early[2], "col", 1)
    quarter = share_of_sum(grad_probe, weight)
    quarter, returned_early = lax.optimization_barrier((quarter, returned_early))
    back_early = shifted(early[1].at[:, :, :, :N].add(returned_early[:, :, TILE:]), "row", 1)
    quarter, back_late = lax.optimization_barrier((sum_plane(quarter), back_late))
    half = gather_half(probe, quarter)
    half, back_early = lax.optimization_barrier((half, back_early))
    tiles = []
    for own, returned, back in ((early[0], returned_early, back_early), (late[0], returned_late, back_late)):
        own = own.at[:, :, :, :N].add(returned[:, :, :TILE])
        tiles.append(own.at[:, :, :N, :].add(back))
    new_object = object_field - STEP_OBJECT * jnp.concatenate(tiles, axis=1)
    return new_object, gather_whole(half).reshape(probe.shape)


def solution(mesh):
    mapped = jax.shard_map(
        shards,
        mesh=mesh,
        in_specs=(
            P(),
            P(None, None, "row", "col"),
            P(),
            P("row", "col", None, None, None),
            P("row", "col", None, None),
            P("row", "col"),
        ),
        out_specs=(P(None, None, "row", "col"), P()),
        check_vma=False,
    )
    return partial(mapped, jnp.asarray(tables_np()))
```

```python
from functools import partial
import math

import jax
import jax.numpy as jnp
import ml_dtypes
import numpy as np
from jax import lax
from jax.experimental import pallas as pl
from jax.experimental.pallas import tpu as pltpu
from jax.sharding import PartitionSpec as P

FRESNEL = 4.0
STEP_OBJECT = 0.5
STEP_PROBE = 0.5
AXES = ("row", "col")
N = 128
MODES = 4
EXT = 384
TILE = 256
VMEM_LIMIT = 50 * 1024 * 1024


def split_np(matrix):
    high = matrix.astype(np.float32).astype(ml_dtypes.bfloat16)
    low = (matrix - high.astype(np.float64)).astype(np.float32).astype(ml_dtypes.bfloat16)
    return np.stack([high, low])


def tables_np():
    position = np.arange(N)
    dft = np.exp(-2j * np.pi * (np.outer(position, position) % N) / N) / math.sqrt(N)
    frequency = np.where(position < N // 2, position, position - N) / N
    chirp = np.exp(-1j * np.pi * FRESNEL * frequency**2)
    propagator = dft.conj() @ (chirp[:, None] * dft)
    propagator = 0.5 * (propagator + propagator.T)
    out = []
    for matrix in (propagator, dft):
        real, imag = matrix.real, matrix.imag
        out.append(
            np.stack(
                [
                    split_np(np.block([[real, imag], [-imag, real]])),
                    split_np(np.block([[real, -imag], [imag, real]])),
                ]
            )
        )
    return np.stack(out)


def split(value):
    high = value.astype(jnp.bfloat16)
    low = (value - high.astype(jnp.float32)).astype(jnp.bfloat16)
    return high, low


def dot(left, right):
    return jnp.dot(left, right, preferred_element_type=jnp.float32)


def sandwich(waves, tables, which, conj):
    right_form, left_form = (1, 0) if conj else (0, 1)
    high, low = tables[which, right_form, 0], tables[which, right_form, 1]
    right = jnp.concatenate([high, high, low], axis=0)
    high, low = tables[which, left_form, 0], tables[which, left_form, 1]
    left = jnp.concatenate([high, high, low], axis=1)
    mixed = []
    for wave in waves:
        high, low = split(jnp.concatenate(wave, axis=1))
        mixed.append(dot(jnp.concatenate([high, low, high], axis=1), right))
    out = []
    for first in range(0, MODES, 2):
        pair = mixed[first : first + 2]
        high, low = split(
            jnp.concatenate(
                [
                    jnp.concatenate([wave[:, :N] for wave in pair], axis=1),
                    jnp.concatenate([wave[:, N:] for wave in pair], axis=1),
                ],
                axis=0,
            )
        )
        operand = jnp.concatenate([high, low, high], axis=0)
        real, imag = dot(left[:N], operand), dot(left[N:], operand)
        out += [(real[:, :N], imag[:, :N]), (real[:, N:], imag[:, N:])]
    return out


def load_waves(ref):
    return [(ref[0, m * N : (m + 1) * N], ref[1, m * N : (m + 1) * N]) for m in range(MODES)]


def store_waves(ref, waves):
    for m, (real, imag) in enumerate(waves):
        ref[0, m * N : (m + 1) * N] = real
        ref[1, m * N : (m + 1) * N] = imag


def times(waves, other):
    a, b = other
    return [(real * a - imag * b, real * b + imag * a) for real, imag in waves]


def times_conj(waves, other):
    a, b = other
    return [(real * a + imag * b, imag * a - real * b) for real, imag in waves]


def sum_modes(terms):
    return (terms[0] + terms[1]) + (terms[2] + terms[3])


def slice_gradient(waves, grads):
    pairs = [(*wave, *grad) for wave, grad in zip(waves, grads)]
    return (
        sum_modes([a * c + b * d for a, b, c, d in pairs]),
        sum_modes([a * d - b * c for a, b, c, d in pairs]),
    )


def corner_of(place, slot):
    row, col = place[slot, 0], place[slot, 1]
    tile = jnp.where(col >= N, 1, 0)
    return row, tile, col - tile * N


def cut(ext, part, depth, where):
    row, tile, turn = where
    block = jnp.concatenate([ext[part, depth, tile + k, pl.ds(row, N), :] for k in range(2)], axis=1)
    return pltpu.roll(block, lax.rem(2 * N - turn, 2 * N), 1)[:, :N]


def deposit(ext, part, depth, where, value):
    row, tile, turn = where
    block = pltpu.roll(jnp.concatenate([value, jnp.zeros_like(value)], axis=1), turn, 1)
    for k in range(2):
        ext[part, depth, tile + k, pl.ds(row, N), :] += block[:, k * N : (k + 1) * N]


def run_copies(pairs, sems):
    copies = [pltpu.make_async_copy(*pair, sems.at[k]) for k, pair in enumerate(pairs)]
    for copy in copies:
        copy.start()
    for copy in copies:
        copy.wait()


def load_extended(first, own, bottom, right, corner, ext, sems):
    upper, lower = pl.ds(0, TILE), pl.ds(TILE, N)
    pairs = []
    for k in range(2):
        lanes = pl.ds(k * N, N)
        pairs.append((own.at[:, pl.ds(first, 2), :, lanes], ext.at[:, :, k, upper]))
        pairs.append((bottom.at[:, :, :, lanes], ext.at[:, :, k, lower]))
    pairs.append((right, ext.at[:, :, 2, upper]))
    pairs.append((corner, ext.at[:, :, 2, lower]))
    run_copies(pairs, sems)


def store_gradient(ext, own, bottom, right, sems):
    pairs = []
    for k in range(2):
        lanes = pl.ds(k * N, N)
        pairs.append((ext.at[:, :, k, pl.ds(0, TILE)], own.at[:, :, :, lanes]))
        pairs.append((ext.at[:, :, k, pl.ds(TILE, N)], bottom.at[:, :, :, lanes]))
    pairs.append((ext.at[:, :, 2], right))
    run_copies(pairs, sems)


def cut_slice(ext, depth, where):
    return cut(ext, 0, depth, where), cut(ext, 1, depth, where)


def deposit_slice(grad, depth, where, value):
    deposit(grad, 0, depth, where, value[0])
    deposit(grad, 1, depth, where, value[1])


def first_half(place, count, own, bottom, right, corner, probe, tables, windows, wave1, wave2, weight, ext, sems):
    slot = pl.program_id(0)

    @pl.when(slot == 0)
    def _():
        load_extended(0, own, bottom, right, corner, ext, sems)
        weight[...] = jnp.zeros_like(weight)

    @pl.when(slot < count[0])
    def _():
        where = corner_of(place, slot)
        waves = load_waves(probe)
        for depth in range(2):
            window = cut_slice(ext, depth, where)
            windows[0, 0, depth], windows[0, 1, depth] = window
            if depth == 0:
                weight[...] += window[0] * window[0] + window[1] * window[1]
            waves = sandwich(times(waves, window), tables, 0, False)
            store_waves((wave1, wave2)[depth].at[0], waves)


def second_half(
    place, count, own, bottom, right, corner, wave2, amplitude, tables, grad2, grad_own, grad_bottom, grad_right, ext, grad, wave3, sems
):
    slot = pl.program_id(0)

    @pl.when(slot == 0)
    def _():
        load_extended(2, own, bottom, right, corner, ext, sems)
        grad[...] = jnp.zeros_like(grad)

    @pl.when(slot < count[0])
    def _():
        where = corner_of(place, slot)
        object2, object3 = cut_slice(ext, 0, where), cut_slice(ext, 1, where)
        waves = sandwich(times(load_waves(wave2.at[0]), object2), tables, 0, False)
        store_waves(wave3, waves)
        far = sandwich(times(waves, object3), tables, 1, False)
        intensity = sum_modes([real * real + imag * imag for real, imag in far])
        factor = 2.0 - 2.0 * (amplitude[0] / jnp.sqrt(intensity + 1.0))
        grads = sandwich([(real * factor, imag * factor) for real, imag in far], tables, 1, True)
        deposit_slice(grad, 1, where, slice_gradient(load_waves(wave3), grads))
        grads = sandwich(times_conj(grads, object3), tables, 0, True)
        deposit_slice(grad, 0, where, slice_gradient(load_waves(wave2.at[0]), grads))
        store_waves(grad2.at[0], times_conj(grads, object2))

    @pl.when(slot == pl.num_programs(0) - 1)
    def _():
        store_gradient(grad, grad_own, grad_bottom, grad_right, sems)


def third_part(place, count, windows, wave1, grad2, probe, tables, grad_probe, grad_own, grad_bottom, grad_right, grad, sems):
    slot = pl.program_id(0)

    @pl.when(slot == 0)
    def _():
        grad[...] = jnp.zeros_like(grad)
        grad_probe[...] = jnp.zeros_like(grad_probe)

    @pl.when(slot < count[0])
    def _():
        where = corner_of(place, slot)
        object0, object1 = [(windows[0, 0, depth], windows[0, 1, depth]) for depth in range(2)]
        grads = sandwich(load_waves(grad2.at[0]), tables, 0, True)
        deposit_slice(grad, 1, where, slice_gradient(load_waves(wave1.at[0]), grads))
        grads = sandwich(times_conj(grads, object1), tables, 0, True)
        deposit_slice(grad, 0, where, slice_gradient(load_waves(probe), grads))
        for m, (real, imag) in enumerate(times_conj(grads, object0)):
            grad_probe[0, m * N : (m + 1) * N] += real
            grad_probe[1, m * N : (m + 1) * N] += imag

    @pl.when(slot == pl.num_programs(0) - 1)
    def _():
        store_gradient(grad, grad_own, grad_bottom, grad_right, sems)


def cost(products):
    flops = products * 5 * 3 * 2 * MODES * N * (2 * N) * (2 * N)
    return pl.CostEstimate(flops=2 * flops, bytes_accessed=8 * 2**20, transcendentals=0)


def f32(*shape):
    return jax.ShapeDtypeStruct(shape, jnp.float32)


def whole(*shape):
    return pl.BlockSpec(shape, lambda slot: (0,) * len(shape))


def per_slot(*shape):
    return pl.BlockSpec((1, *shape), lambda slot: (slot,) + (0,) * len(shape))


SMEM = pl.BlockSpec(memory_space=pltpu.SMEM)
HBM = pl.BlockSpec(memory_space=pl.ANY)
PARAMS = pltpu.CompilerParams(vmem_limit_bytes=VMEM_LIMIT, dimension_semantics=("arbitrary",))
TABLES = whole(2, 2, 2, 2 * N, 2 * N)
WAVE = (2, MODES * N, N)
EXTENDED = pltpu.VMEM((2, 2, 3, EXT, N), jnp.float32)


def shifted(value, axis, steps):
    count = lax.axis_size(axis)
    leading, last = (max(0, -steps), min(count, count - steps))
    return lax.ppermute(value, axis, [(source, source + steps) for source in range(leading, last)])


def diagonal(value):
    rows, cols = lax.axis_size("row"), lax.axis_size("col")
    pairs = [(a * cols + b, (a - 1) * cols + b - 1) for a in range(1, rows) for b in range(1, cols)]
    return lax.ppermute(value, AXES, pairs)


def mesh_perm(move):
    pairs = []
    for z in range(4):
        for x in range(4):
            for y in range(4):
                for core in range(2):
                    to_z, to_x, to_y, to_core = move(z, x, y, core)
                    source = z * 32 + (x * 4 + y) * 2 + core
                    pairs.append((source, to_z * 32 + (to_x * 4 + to_y) * 2 + to_core))
    return pairs


SWAP_CORE = mesh_perm(lambda z, x, y, core: (z, x, y, 1 - core))
ALONG_Z = {k: mesh_perm(lambda z, x, y, core, k=k: (z ^ k, x, y, core)) for k in (1, 2, 3)}
ALONG_X = {k: mesh_perm(lambda z, x, y, core, k=k: (z, x ^ k, y, core)) for k in (1, 2, 3)}
ALONG_Y = {k: mesh_perm(lambda z, x, y, core, k=k: (z, x, y ^ k, core)) for k in (1, 2, 3)}


QUARTER = N // 8


def part(value, index, size):
    return lax.dynamic_slice_in_dim(value, index * size, size, axis=1)


def share_of_sum(grad_probe, weight):
    z = lax.axis_index("row")
    core = lax.axis_index("col") % 2
    total = jnp.concatenate([grad_probe.reshape(2 * MODES, N, N), weight[None]], axis=0)
    rows = N // 2
    total = part(total, core, rows) + lax.ppermute(part(total, 1 - core, rows), AXES, SWAP_CORE)
    arrived = [lax.ppermute(part(total, z ^ k, QUARTER), AXES, ALONG_Z[k]) for k in (1, 2, 3)]
    return part(total, z, QUARTER) + arrived[0] + arrived[1] + arrived[2]


def sum_plane(total):
    for along in (ALONG_Y, ALONG_X):
        arrived = [total] + [lax.ppermute(total, AXES, along[k]) for k in (1, 2, 3)]
        total = (arrived[0] + arrived[1]) + (arrived[2] + arrived[3])
    return total


def gather_half(probe, total):
    z = lax.axis_index("row")
    core = lax.axis_index("col") % 2
    mine = part(probe.reshape(2 * MODES, N, N), core * 4 + z, QUARTER)
    mine = mine - STEP_PROBE * total[: 2 * MODES] / (total[2 * MODES :] + 1.0)
    arrived = [mine] + [lax.ppermute(mine, AXES, ALONG_Z[k]) for k in (1, 2, 3)]
    half = jnp.zeros((2 * MODES, N // 2, N), jnp.float32)
    for k in range(4):
        half = lax.dynamic_update_slice_in_dim(half, arrived[k], (z ^ k) * QUARTER, axis=1)
    return half


def gather_whole(half):
    core = lax.axis_index("col") % 2
    other = lax.ppermute(half, AXES, SWAP_CORE)
    low = jnp.where(core == 0, half, other)
    high = jnp.where(core == 0, other, half)
    return jnp.concatenate([low, high], axis=1)


def shards(tables, object_field, probe, amplitudes, offsets, counts):
    row_index = lax.axis_index("row")
    col_index = lax.axis_index("col")
    slots = offsets.shape[2]
    origin = jnp.stack([row_index * TILE, col_index * TILE]).astype(jnp.int32)
    place = offsets[0, 0] - origin[None, :]
    count = counts[0]
    waves = probe.reshape(WAVE)

    bottoms, rights = [], []
    for first in (0, 2):
        piece = object_field[:, first : first + 2]
        bottoms.append(shifted(piece[:, :, :N, :], "row", -1))
        rights.append(shifted(piece[:, :, :, :N], "col", -1))

    corners = [shifted(bottoms[0][:, :, :, :N], "col", -1), diagonal(object_field[:, 2:, :N, :N])]

    windows, wave1, wave2, weight = pl.pallas_call(
        first_half,
        grid=(slots,),
        in_specs=[SMEM, SMEM, HBM, HBM, HBM, HBM, whole(*WAVE), TABLES],
        out_specs=[per_slot(2, 2, N, N), per_slot(*WAVE), per_slot(*WAVE), whole(N, N)],
        out_shape=[f32(slots, 2, 2, N, N), f32(slots, *WAVE), f32(slots, *WAVE), f32(N, N)],
        scratch_shapes=[EXTENDED, pltpu.SemaphoreType.DMA((6,))],
        compiler_params=PARAMS,
        cost_estimate=cost(4),
        name="first_half",
    )(place, count, object_field, bottoms[0], rights[0], corners[0], waves, tables)

    wave2, bottoms[1] = lax.optimization_barrier((wave2, bottoms[1]))
    grad_specs = [HBM, HBM, HBM]
    grad_shapes = [f32(2, 2, TILE, TILE), f32(2, 2, N, TILE), f32(2, 2, EXT, N)]
    grad2, *late = pl.pallas_call(
        second_half,
        grid=(slots,),
        in_specs=[SMEM, SMEM, HBM, HBM, HBM, HBM, per_slot(*WAVE), per_slot(N, N), TABLES],
        out_specs=[per_slot(*WAVE)] + grad_specs,
        out_shape=[f32(slots, *WAVE)] + grad_shapes,
        scratch_shapes=[EXTENDED, EXTENDED, pltpu.VMEM(WAVE, jnp.float32), pltpu.SemaphoreType.DMA((6,))],
        compiler_params=PARAMS,
        cost_estimate=cost(8),
        name="second_half",
    )(place, count, object_field, bottoms[1], rights[1], corners[1], wave2, amplitudes[0, 0], tables)

    grad_probe, *early = pl.pallas_call(
        third_part,
        grid=(slots,),
        in_specs=[SMEM, SMEM, per_slot(2, 2, N, N), per_slot(*WAVE), per_slot(*WAVE), whole(*WAVE), TABLES],
        out_specs=[whole(*WAVE)] + grad_specs,
        out_shape=[f32(*WAVE)] + grad_shapes,
        scratch_shapes=[EXTENDED, pltpu.SemaphoreType.DMA((5,))],
        compiler_params=PARAMS,
        cost_estimate=cost(4),
        name="third_part",
    )(place, count, windows, wave1, grad2, waves, tables)

    returned_late = shifted(late[2], "col", 1)
    grad_probe, returned_late = lax.optimization_barrier((grad_probe, returned_late))
    back_late = shifted(late[1].at[:, :, :, :N].add(returned_late[:, :, TILE:]), "row", 1)
    returned_early = shifted(early[2], "col", 1)
    quarter = share_of_sum(grad_probe, weight)
    quarter, returned_early = lax.optimization_barrier((quarter, returned_early))
    back_early = shifted(early[1].at[:, :, :, :N].add(returned_early[:, :, TILE:]), "row", 1)
    quarter, back_late = lax.optimization_barrier((sum_plane(quarter), back_late))
    half = gather_half(probe, quarter)
    half, back_early = lax.optimization_barrier((half, back_early))
    tiles = []
    for own, returned, back in ((early[0], returned_early, back_early), (late[0], returned_late, back_late)):
        own = own.at[:, :, :, :N].add(returned[:, :, :TILE])
        tiles.append(own.at[:, :, :N, :].add(back))
    new_object = object_field - STEP_OBJECT * jnp.concatenate(tiles, axis=1)
    return new_object, gather_whole(half).reshape(probe.shape)


def solution(mesh):
    mapped = jax.shard_map(
        shards,
        mesh=mesh,
        in_specs=(
            P(),
            P(None, None, "row", "col"),
            P(),
            P("row", "col", None, None, None),
            P("row", "col", None, None),
            P("row", "col"),
        ),
        out_specs=(P(None, None, "row", "col"), P()),
        check_vma=False,
    )
    return partial(mapped, jnp.asarray(tables_np()))
```

```python
from functools import partial
import math

import jax
import jax.numpy as jnp
import ml_dtypes
import numpy as np
from jax import lax
from jax.experimental import pallas as pl
from jax.experimental.pallas import tpu as pltpu
from jax.sharding import PartitionSpec as P

FRESNEL = 4.0
STEP_OBJECT = 0.5
STEP_PROBE = 0.5
AXES = ("row", "col")
N = 128
MODES = 4
EXT = 384
TILE = 256
VMEM_LIMIT = 50 * 1024 * 1024


def split_np(matrix):
    high = matrix.astype(np.float32).astype(ml_dtypes.bfloat16)
    low = (matrix - high.astype(np.float64)).astype(np.float32).astype(ml_dtypes.bfloat16)
    return np.stack([high, low])


def tables_np():
    position = np.arange(N)
    dft = np.exp(-2j * np.pi * (np.outer(position, position) % N) / N) / math.sqrt(N)
    frequency = np.where(position < N // 2, position, position - N) / N
    chirp = np.exp(-1j * np.pi * FRESNEL * frequency**2)
    propagator = dft.conj() @ (chirp[:, None] * dft)
    propagator = 0.5 * (propagator + propagator.T)
    out = []
    for matrix in (propagator, dft):
        real, imag = matrix.real, matrix.imag
        out.append(
            np.stack(
                [
                    split_np(np.block([[real, imag], [-imag, real]])),
                    split_np(np.block([[real, -imag], [imag, real]])),
                ]
            )
        )
    return np.stack(out)


def split(value):
    high = value.astype(jnp.bfloat16)
    low = (value - high.astype(jnp.float32)).astype(jnp.bfloat16)
    return high, low


def dot(left, right):
    return jnp.dot(left, right, preferred_element_type=jnp.float32)


def sandwich(waves, tables, which, conj):
    right_form, left_form = (1, 0) if conj else (0, 1)
    high, low = tables[which, right_form, 0], tables[which, right_form, 1]
    right = jnp.concatenate([high, high, low], axis=0)
    high, low = tables[which, left_form, 0], tables[which, left_form, 1]
    left = jnp.concatenate([high, high, low], axis=1)
    mixed = []
    for wave in waves:
        high, low = split(jnp.concatenate(wave, axis=1))
        mixed.append(dot(jnp.concatenate([high, low, high], axis=1), right))
    out = []
    for first in range(0, MODES, 2):
        pair = mixed[first : first + 2]
        high, low = split(
            jnp.concatenate(
                [
                    jnp.concatenate([wave[:, :N] for wave in pair], axis=1),
                    jnp.concatenate([wave[:, N:] for wave in pair], axis=1),
                ],
                axis=0,
            )
        )
        operand = jnp.concatenate([high, low, high], axis=0)
        real, imag = dot(left[:N], operand), dot(left[N:], operand)
        out += [(real[:, :N], imag[:, :N]), (real[:, N:], imag[:, N:])]
    return out


def load_waves(ref):
    return [(ref[0, m * N : (m + 1) * N], ref[1, m * N : (m + 1) * N]) for m in range(MODES)]


def store_waves(ref, waves):
    for m, (real, imag) in enumerate(waves):
        ref[0, m * N : (m + 1) * N] = real
        ref[1, m * N : (m + 1) * N] = imag


def times(waves, other):
    a, b = other
    return [(real * a - imag * b, real * b + imag * a) for real, imag in waves]


def times_conj(waves, other):
    a, b = other
    return [(real * a + imag * b, imag * a - real * b) for real, imag in waves]


def sum_modes(terms):
    return (terms[0] + terms[1]) + (terms[2] + terms[3])


def slice_gradient(waves, grads):
    pairs = [(*wave, *grad) for wave, grad in zip(waves, grads)]
    return (
        sum_modes([a * c + b * d for a, b, c, d in pairs]),
        sum_modes([a * d - b * c for a, b, c, d in pairs]),
    )


def corner_of(place, slot):
    row, col = place[slot, 0], place[slot, 1]
    tile = jnp.where(col >= N, 1, 0)
    return row, tile, col - tile * N


def cut(ext, part, depth, where):
    row, tile, turn = where
    block = jnp.concatenate([ext[part, depth, tile + k, pl.ds(row, N), :] for k in range(2)], axis=1)
    return pltpu.roll(block, lax.rem(2 * N - turn, 2 * N), 1)[:, :N]


def deposit(ext, part, depth, where, value):
    row, tile, turn = where
    block = pltpu.roll(jnp.concatenate([value, jnp.zeros_like(value)], axis=1), turn, 1)
    for k in range(2):
        ext[part, depth, tile + k, pl.ds(row, N), :] += block[:, k * N : (k + 1) * N]


def run_copies(pairs, sems, zeroed=None):
    copies = [pltpu.make_async_copy(*pair, sems.at[k]) for k, pair in enumerate(pairs)]
    for copy in copies:
        copy.start()
    if zeroed is not None:
        zeroed[...] = jnp.zeros_like(zeroed)
    for copy in copies:
        copy.wait()


def load_extended(first, own, bottom, right, corner, ext, sems, zeroed=None):
    upper, lower = pl.ds(0, TILE), pl.ds(TILE, N)
    pairs = []
    for k in range(2):
        lanes = pl.ds(k * N, N)
        pairs.append((own.at[:, pl.ds(first, 2), :, lanes], ext.at[:, :, k, upper]))
        pairs.append((bottom.at[:, :, :, lanes], ext.at[:, :, k, lower]))
    pairs.append((right, ext.at[:, :, 2, upper]))
    pairs.append((corner, ext.at[:, :, 2, lower]))
    run_copies(pairs, sems, zeroed)


def store_gradient(ext, own, bottom, right, sems):
    pairs = []
    for k in range(2):
        lanes = pl.ds(k * N, N)
        pairs.append((ext.at[:, :, k, pl.ds(0, TILE)], own.at[:, :, :, lanes]))
        pairs.append((ext.at[:, :, k, pl.ds(TILE, N)], bottom.at[:, :, :, lanes]))
    pairs.append((ext.at[:, :, 2], right))
    run_copies(pairs, sems)


def cut_slice(ext, depth, where):
    return cut(ext, 0, depth, where), cut(ext, 1, depth, where)


def deposit_slice(grad, depth, where, value):
    deposit(grad, 0, depth, where, value[0])
    deposit(grad, 1, depth, where, value[1])


def first_half(place, count, own, bottom, right, corner, probe, tables, windows, wave1, wave2, weight, ext, sems):
    slot = pl.program_id(0)

    @pl.when(slot == 0)
    def _():
        load_extended(0, own, bottom, right, corner, ext, sems, weight)

    @pl.when(slot < count[0])
    def _():
        where = corner_of(place, slot)
        waves = load_waves(probe)
        for depth in range(2):
            window = cut_slice(ext, depth, where)
            windows[0, 0, depth], windows[0, 1, depth] = window
            if depth == 0:
                weight[...] += window[0] * window[0] + window[1] * window[1]
            waves = sandwich(times(waves, window), tables, 0, False)
            store_waves((wave1, wave2)[depth].at[0], waves)


def second_half(
    place, count, own, bottom, right, corner, wave2, amplitude, tables, grad2, grad_own, grad_bottom, grad_right, ext, grad, wave3, sems
):
    slot = pl.program_id(0)

    @pl.when(slot == 0)
    def _():
        load_extended(2, own, bottom, right, corner, ext, sems, grad)

    @pl.when(slot < count[0])
    def _():
        where = corner_of(place, slot)
        object2, object3 = cut_slice(ext, 0, where), cut_slice(ext, 1, where)
        waves = sandwich(times(load_waves(wave2.at[0]), object2), tables, 0, False)
        store_waves(wave3, waves)
        far = sandwich(times(waves, object3), tables, 1, False)
        intensity = sum_modes([real * real + imag * imag for real, imag in far])
        factor = 2.0 - 2.0 * (amplitude[0] / jnp.sqrt(intensity + 1.0))
        grads = sandwich([(real * factor, imag * factor) for real, imag in far], tables, 1, True)
        deposit_slice(grad, 1, where, slice_gradient(load_waves(wave3), grads))
        grads = sandwich(times_conj(grads, object3), tables, 0, True)
        deposit_slice(grad, 0, where, slice_gradient(load_waves(wave2.at[0]), grads))
        store_waves(grad2.at[0], times_conj(grads, object2))

    @pl.when(slot == pl.num_programs(0) - 1)
    def _():
        store_gradient(grad, grad_own, grad_bottom, grad_right, sems)


def third_part(place, count, windows, wave1, grad2, probe, tables, grad_probe, grad_own, grad_bottom, grad_right, grad, sems):
    slot = pl.program_id(0)

    @pl.when(slot == 0)
    def _():
        grad[...] = jnp.zeros_like(grad)
        grad_probe[...] = jnp.zeros_like(grad_probe)

    @pl.when(slot < count[0])
    def _():
        where = corner_of(place, slot)
        object0, object1 = [(windows[0, 0, depth], windows[0, 1, depth]) for depth in range(2)]
        grads = sandwich(load_waves(grad2.at[0]), tables, 0, True)
        deposit_slice(grad, 1, where, slice_gradient(load_waves(wave1.at[0]), grads))
        grads = sandwich(times_conj(grads, object1), tables, 0, True)
        deposit_slice(grad, 0, where, slice_gradient(load_waves(probe), grads))
        for m, (real, imag) in enumerate(times_conj(grads, object0)):
            grad_probe[0, m * N : (m + 1) * N] += real
            grad_probe[1, m * N : (m + 1) * N] += imag

    @pl.when(slot == pl.num_programs(0) - 1)
    def _():
        store_gradient(grad, grad_own, grad_bottom, grad_right, sems)


def cost(products):
    flops = products * 5 * 3 * 2 * MODES * N * (2 * N) * (2 * N)
    return pl.CostEstimate(flops=2 * flops, bytes_accessed=8 * 2**20, transcendentals=0)


def f32(*shape):
    return jax.ShapeDtypeStruct(shape, jnp.float32)


def whole(*shape):
    return pl.BlockSpec(shape, lambda slot: (0,) * len(shape))


def per_slot(*shape):
    return pl.BlockSpec((1, *shape), lambda slot: (slot,) + (0,) * len(shape))


SMEM = pl.BlockSpec(memory_space=pltpu.SMEM)
HBM = pl.BlockSpec(memory_space=pl.ANY)
PARAMS = pltpu.CompilerParams(vmem_limit_bytes=VMEM_LIMIT, dimension_semantics=("arbitrary",))
TABLES = whole(2, 2, 2, 2 * N, 2 * N)
WAVE = (2, MODES * N, N)
EXTENDED = pltpu.VMEM((2, 2, 3, EXT, N), jnp.float32)


def shifted(value, axis, steps):
    count = lax.axis_size(axis)
    leading, last = (max(0, -steps), min(count, count - steps))
    return lax.ppermute(value, axis, [(source, source + steps) for source in range(leading, last)])


def diagonal(value):
    rows, cols = lax.axis_size("row"), lax.axis_size("col")
    pairs = [(a * cols + b, (a - 1) * cols + b - 1) for a in range(1, rows) for b in range(1, cols)]
    return lax.ppermute(value, AXES, pairs)


def mesh_perm(move):
    pairs = []
    for z in range(4):
        for x in range(4):
            for y in range(4):
                for core in range(2):
                    to_z, to_x, to_y, to_core = move(z, x, y, core)
                    source = z * 32 + (x * 4 + y) * 2 + core
                    pairs.append((source, to_z * 32 + (to_x * 4 + to_y) * 2 + to_core))
    return pairs


SWAP_CORE = mesh_perm(lambda z, x, y, core: (z, x, y, 1 - core))
ALONG_Z = {k: mesh_perm(lambda z, x, y, core, k=k: (z ^ k, x, y, core)) for k in (1, 2, 3)}
ALONG_X = {k: mesh_perm(lambda z, x, y, core, k=k: (z, x ^ k, y, core)) for k in (1, 2, 3)}
ALONG_Y = {k: mesh_perm(lambda z, x, y, core, k=k: (z, x, y ^ k, core)) for k in (1, 2, 3)}


QUARTER = N // 8


def part(value, index, size):
    return lax.dynamic_slice_in_dim(value, index * size, size, axis=1)


def share_of_sum(grad_probe, weight):
    z = lax.axis_index("row")
    core = lax.axis_index("col") % 2
    total = jnp.concatenate([grad_probe.reshape(2 * MODES, N, N), weight[None]], axis=0)
    rows = N // 2
    total = part(total, core, rows) + lax.ppermute(part(total, 1 - core, rows), AXES, SWAP_CORE)
    arrived = [lax.ppermute(part(total, z ^ k, QUARTER), AXES, ALONG_Z[k]) for k in (1, 2, 3)]
    return part(total, z, QUARTER) + arrived[0] + arrived[1] + arrived[2]


def sum_plane(total):
    for along in (ALONG_Y, ALONG_X):
        arrived = [total] + [lax.ppermute(total, AXES, along[k]) for k in (1, 2, 3)]
        total = (arrived[0] + arrived[1]) + (arrived[2] + arrived[3])
    return total


def gather_half(probe, total):
    z = lax.axis_index("row")
    core = lax.axis_index("col") % 2
    mine = part(probe.reshape(2 * MODES, N, N), core * 4 + z, QUARTER)
    mine = mine - STEP_PROBE * total[: 2 * MODES] / (total[2 * MODES :] + 1.0)
    arrived = [mine] + [lax.ppermute(mine, AXES, ALONG_Z[k]) for k in (1, 2, 3)]
    half = jnp.zeros((2 * MODES, N // 2, N), jnp.float32)
    for k in range(4):
        half = lax.dynamic_update_slice_in_dim(half, arrived[k], (z ^ k) * QUARTER, axis=1)
    return half


def gather_whole(half):
    core = lax.axis_index("col") % 2
    other = lax.ppermute(half, AXES, SWAP_CORE)
    low = jnp.where(core == 0, half, other)
    high = jnp.where(core == 0, other, half)
    return jnp.concatenate([low, high], axis=1)


def shards(tables, object_field, probe, amplitudes, offsets, counts):
    row_index = lax.axis_index("row")
    col_index = lax.axis_index("col")
    slots = offsets.shape[2]
    origin = jnp.stack([row_index * TILE, col_index * TILE]).astype(jnp.int32)
    place = offsets[0, 0] - origin[None, :]
    count = counts[0]
    waves = probe.reshape(WAVE)

    bottoms, rights = [], []
    for first in (0, 2):
        piece = object_field[:, first : first + 2]
        bottoms.append(shifted(piece[:, :, :N, :], "row", -1))
        rights.append(shifted(piece[:, :, :, :N], "col", -1))

    corners = [shifted(bottoms[0][:, :, :, :N], "col", -1), diagonal(object_field[:, 2:, :N, :N])]

    windows, wave1, wave2, weight = pl.pallas_call(
        first_half,
        grid=(slots,),
        in_specs=[SMEM, SMEM, HBM, HBM, HBM, HBM, whole(*WAVE), TABLES],
        out_specs=[per_slot(2, 2, N, N), per_slot(*WAVE), per_slot(*WAVE), whole(N, N)],
        out_shape=[f32(slots, 2, 2, N, N), f32(slots, *WAVE), f32(slots, *WAVE), f32(N, N)],
        scratch_shapes=[EXTENDED, pltpu.SemaphoreType.DMA((6,))],
        compiler_params=PARAMS,
        cost_estimate=cost(4),
        name="first_half",
    )(place, count, object_field, bottoms[0], rights[0], corners[0], waves, tables)

    wave2, bottoms[1] = lax.optimization_barrier((wave2, bottoms[1]))
    grad_specs = [HBM, HBM, HBM]
    grad_shapes = [f32(2, 2, TILE, TILE), f32(2, 2, N, TILE), f32(2, 2, EXT, N)]
    grad2, *late = pl.pallas_call(
        second_half,
        grid=(slots,),
        in_specs=[SMEM, SMEM, HBM, HBM, HBM, HBM, per_slot(*WAVE), per_slot(N, N), TABLES],
        out_specs=[per_slot(*WAVE)] + grad_specs,
        out_shape=[f32(slots, *WAVE)] + grad_shapes,
        scratch_shapes=[EXTENDED, EXTENDED, pltpu.VMEM(WAVE, jnp.float32), pltpu.SemaphoreType.DMA((6,))],
        compiler_params=PARAMS,
        cost_estimate=cost(8),
        name="second_half",
    )(place, count, object_field, bottoms[1], rights[1], corners[1], wave2, amplitudes[0, 0], tables)

    grad_probe, *early = pl.pallas_call(
        third_part,
        grid=(slots,),
        in_specs=[SMEM, SMEM, per_slot(2, 2, N, N), per_slot(*WAVE), per_slot(*WAVE), whole(*WAVE), TABLES],
        out_specs=[whole(*WAVE)] + grad_specs,
        out_shape=[f32(*WAVE)] + grad_shapes,
        scratch_shapes=[EXTENDED, pltpu.SemaphoreType.DMA((5,))],
        compiler_params=PARAMS,
        cost_estimate=cost(4),
        name="third_part",
    )(place, count, windows, wave1, grad2, waves, tables)

    returned_late = shifted(late[2], "col", 1)
    grad_probe, returned_late = lax.optimization_barrier((grad_probe, returned_late))
    back_late = shifted(late[1].at[:, :, :, :N].add(returned_late[:, :, TILE:]), "row", 1)
    returned_early = shifted(early[2], "col", 1)
    quarter = share_of_sum(grad_probe, weight)
    quarter, returned_early = lax.optimization_barrier((quarter, returned_early))
    back_early = shifted(early[1].at[:, :, :, :N].add(returned_early[:, :, TILE:]), "row", 1)
    quarter, back_late = lax.optimization_barrier((sum_plane(quarter), back_late))
    half = gather_half(probe, quarter)
    half, back_early = lax.optimization_barrier((half, back_early))
    tiles = []
    for own, returned, back in ((early[0], returned_early, back_early), (late[0], returned_late, back_late)):
        own = own.at[:, :, :, :N].add(returned[:, :, :TILE])
        tiles.append(own.at[:, :, :N, :].add(back))
    new_object = object_field - STEP_OBJECT * jnp.concatenate(tiles, axis=1)
    return new_object, gather_whole(half).reshape(probe.shape)


def solution(mesh):
    mapped = jax.shard_map(
        shards,
        mesh=mesh,
        in_specs=(
            P(),
            P(None, None, "row", "col"),
            P(),
            P("row", "col", None, None, None),
            P("row", "col", None, None),
            P("row", "col"),
        ),
        out_specs=(P(None, None, "row", "col"), P()),
        check_vma=False,
    )
    return partial(mapped, jnp.asarray(tables_np()))
```
